256 devices in a mesh: vocab: 64 (over z, x, core), hidden: 4 (over y).
Axes of the slice: x: 4, y: 4, z: 8, core: 2. Of those that a mesh axis runs over, the one named last changes fastest.
Arguments:
- hidden_states: bfloat16 [1024, 3584], P('vocab', 'hidden'), may hold values from -6 to 6
- embedding: bfloat16 [131072, 3584], P('vocab', 'hidden'), may hold values from -9 to 9
- targets: int32 [1024], P('vocab'), may hold values from 0 to 131071
Outputs:
- loss: float32 [], replicated
- hidden_grad: float32 [1024, 3584], P('vocab', 'hidden')
- embedding_grad: float32 [131072, 3584], P('vocab', 'hidden')
The draws below stay inside these ranges and needn't reach their ends.
All inputs are finite; a program needn't handle non-finite values.
Results may differ from the reference program's by a relative error of at most 0.0023.
Values may be sent and summed in bfloat16 or wider, within the bound.
No kernel may reach another device: no remote copies, remote signals or barrier semaphores. Data moves between devices by JAX's collectives and lax.ppermute only.
A program may use at most 128 MiB of HBM per device.

```python
import math
import jax
import jax.numpy as jnp
import numpy as np
from jax import lax

D = 3584
V_DEV = 2048
VOCAB = 131072
TOKENS = 1024
N_VOCAB = 64


def draw_embedding(key, part):
    key = jax.random.fold_in(key, 11)
    key_values, key_rows, key_cols = jax.random.split(key, 3)
    row_scale = jnp.exp(jax.random.uniform(key_rows, (VOCAB, 1), jnp.float32) * jnp.log(10.0))
    col_scale = jnp.exp(jax.random.uniform(key_cols, (1, D), jnp.float32, -1.0, 1.0) * jnp.log(2.0))
    values = jnp.clip(jax.random.normal(key_values, (VOCAB, D), jnp.float32), -6.0, 6.0)
    scaled = 4.0 * D ** (-0.5) * row_scale * col_scale * values
    return jnp.clip(scaled, -9.0, 9.0).astype(jnp.bfloat16)


def plant(array, stream_key, least, largest):
    index_at = [jax.random.randint(jax.random.fold_in(stream_key, axis), (), 0, length) for axis, length in enumerate(array.shape)]
    main_axis = array.shape.index(max(array.shape))
    beside = index_at[:main_axis] + [(index_at[main_axis] + 1) % array.shape[main_axis]] + index_at[main_axis + 1:]
    return array.at[tuple(index_at)].set(least).at[tuple(beside)].set(largest)


def block_levels(rng, dims, cuts, smallest, top_value):
    def one(dim, parts):
        draws = jax.random.uniform(jax.random.fold_in(jax.random.fold_in(rng, 6), dim), (parts,), jnp.float32, smallest / len(cuts), top_value / len(cuts))
        return jnp.repeat(jnp.exp(draws), dims[dim] // parts).reshape((-1,) + (1,) * (len(dims) - dim - 1))

    factor_of = one(*cuts[0])
    for cut in cuts[1:]:
        factor_of = factor_of * one(*cut)
    return factor_of


def wide_ids(key, dims, number_of, skew):
    portions = [min(1 << octave, number_of + 1 - (1 << octave)) * (1 << 20) // math.isqrt((1 << octave) ** skew) + 1 for octave in range((number_of + 1).bit_length()) if 1 << octave <= number_of]
    scale = 1 + sum(portions) // (1 << 30)
    listing = np.cumsum(np.array([max(1, weight // scale) for weight in portions]))
    pick = jax.random.randint(jax.random.fold_in(key, 1), dims, 0, int(listing[len(portions) - 1]))
    start = jnp.left_shift(1, jnp.searchsorted(jnp.asarray(listing, jnp.int32), pick, side="right").astype(jnp.int32))
    standing = start - 1 + jax.random.randint(jax.random.fold_in(key, 4), dims, 0, 1 << 30) % jnp.minimum(start, number_of + 1 - start)
    return jax.random.permutation(jax.random.fold_in(key, 2), number_of)[standing].astype(jnp.int32)


def normal_values(stream_key, shape, deviation, limit, shards=(), held_as=jnp.bfloat16):
    result = jax.random.normal(stream_key, shape, jnp.float32) * deviation
    if len(shards) > 0:
        result = block_levels(stream_key, shape, shards, -0.22, 0.18) * result
    return jnp.clip(result, min=-limit, max=limit).astype(held_as)


def setup_inputs(seed: int = 0) -> dict:
    splits = jax.random.split(jax.random.key(seed), 4)
    hidden_states = normal_values(splits[0], (TOKENS, D), 1.0, 6.0, ((0, 64), (1, 4)))
    embedding = draw_embedding(jax.random.fold_in(splits[3], 71), 0)
    targets = plant(wide_ids(splits[2], (TOKENS,), VOCAB, 2), jax.random.fold_in(splits[2], 3), 0, VOCAB - 1).astype(jnp.int32)
    return dict(hidden_states=hidden_states, embedding=embedding, targets=targets)


soft_ceiling = 30.0


def capped_scores(states, table):
    scores = lax.dot_general(states, table, (((1,), (1,)), ((), ())), preferred_element_type=jnp.float32)
    return soft_ceiling * jnp.tanh(scores / soft_ceiling)


def reference(hidden_states, embedding, targets):
    blocks = embedding.reshape(N_VOCAB, V_DEV, D)
    starts = jnp.arange(N_VOCAB, dtype=jnp.int32) * V_DEV

    def pass_first(running, scanned):
        vocab_block, first_id = scanned
        capped = capped_scores(hidden_states, vocab_block)
        vocab_ids = first_id + jnp.arange(V_DEV, dtype=jnp.int32)
        matches = targets[:, None] == vocab_ids[None, :]
        totals, chosen = running
        totals = totals + jnp.sum(jnp.exp(capped), axis=1)
        chosen = chosen + jnp.sum(jnp.where(matches, capped, jnp.zeros_like(capped)), axis=1)
        return (totals, chosen), None

    empty = jnp.zeros((TOKENS,), jnp.float32)
    (totals, chosen), _ = lax.scan(pass_first, (empty, empty), (blocks, starts))
    loss = jnp.mean(jnp.log(totals) - chosen)

    def pass_second(row_grad, scanned):
        vocab_block, first_id = scanned
        capped = capped_scores(hidden_states, vocab_block)
        vocab_ids = first_id + jnp.arange(V_DEV, dtype=jnp.int32)
        matches = (targets[:, None] == vocab_ids[None, :]).astype(jnp.float32)
        factor = 1.0 - (capped / soft_ceiling) ** 2
        logit_grad = ((jnp.exp(capped) / totals[:, None] - matches) * factor).astype(jnp.bfloat16)
        row_grad = row_grad + jnp.dot(logit_grad, vocab_block, preferred_element_type=jnp.float32)
        table_grad = lax.dot_general(logit_grad, hidden_states, (((0,), (0,)), ((), ())), preferred_element_type=jnp.float32)
        return row_grad, table_grad

    start_grad = jnp.zeros((TOKENS, D), jnp.float32)
    hidden_grad, table_grads = lax.scan(pass_second, start_grad, (blocks, starts))
    return loss, hidden_grad, table_grads.reshape(VOCAB, D)
```

```python
import jax
import jax.numpy as jnp
from jax import lax
from jax.sharding import Mesh, PartitionSpec as P

soft_ceiling = 30.0
swap = [(0, 1), (1, 0)]


def ring(n, s):
    return [(i, (i + s) % n) for i in range(n)]


def over(value, axis, n, s):
    return lax.ppermute(value, axis, ring(n, s))


def ring_sum4(v, axis, roll):
    got = [v] + [jnp.roll(over(v, axis, 4, s), -s, roll) if roll else over(v, axis, 4, s) for s in (1, 2, 3)]
    return (got[0] + got[2]) + (got[1] + got[3])


def local(hidden_states, embedding, targets):
    z, x, c, y = (lax.axis_index(a) for a in ("z", "x", "c", "y"))
    f32, bf16 = jnp.float32, jnp.bfloat16
    rows, width = hidden_states.shape
    entries = embedding.shape[0]
    quarter = entries // 4
    full = 4 * width

    parts = [hidden_states] + [over(hidden_states, "y", 4, s) for s in (1, 2, 3)]
    digits = jnp.stack([targets & 255, (targets >> 8) & 255, targets >> 16], 1).astype(bf16)
    digits = jnp.pad(digits, ((0, 0), (0, 125)))
    block = jnp.concatenate(parts + [digits], 1)

    quarters = embedding.reshape(4, quarter, width)

    def quarter_at(q, k):
        return lax.dynamic_index_in_dim(q, (y + k) % 4, 0, False)

    own = [quarter_at(quarters, 0)] + [over(quarter_at(quarters, s), "y", 4, s) for s in (1, 2, 3)]
    beside = lax.ppermute(embedding, "c", swap).reshape(4, quarter, width)
    other = [quarter_at(beside, 0)] + [lax.ppermute(own[s], "c", swap) for s in (1, 2, 3)]

    at_x = jnp.stack([block] + [over(block, "x", 4, -a) for a in (1, 2, 3)])
    up, down = [at_x], [at_x]
    for _ in range(3):
        up.append(over(up[-1], "z", 8, -1))
        down.append(over(down[-1], "z", 8, 1))
    far = jnp.concatenate([over(up[3][:2], "z", 8, -1), over(down[3][2:], "z", 8, 1)], 0)
    token_rows = jnp.stack(up + [far] + down[:0:-1], 1).reshape(32 * rows, full + 128)
    tokens = 32 * rows
    states = token_rows[:, :full]
    own_states = states[:, :width]
    beside_states = lax.ppermute(own_states, "c", swap)
    dig = token_rows[:, full : full + 3].astype(jnp.int32)
    wanted = dig[:, 0] + dig[:, 1] * 256 + dig[:, 2] * 65536

    table = jnp.concatenate([jnp.concatenate(own, 1), jnp.concatenate(other, 1)], 0)
    logits = lax.dot_general(table, states, (((1,), (1,)), ((), ())), preferred_element_type=f32)
    capped = soft_ceiling * jnp.tanh(logits / soft_ceiling)
    chip = (z * 4 + x) * 2
    ids = jnp.arange(quarter, dtype=jnp.int32) + y * quarter
    ids = jnp.concatenate([(chip + c) * entries + ids, (chip + 1 - c) * entries + ids])
    matches = ids[:, None] == wanted[None, :]
    exponent = jnp.exp(capped)
    sums = jnp.stack([jnp.sum(exponent, 0), jnp.sum(jnp.where(matches, capped, 0.0), 0)])
    sums = sums.reshape(2, 4, 8, rows)
    sums = ring_sum4(sums, "x", 1)
    sums = ring_sum4(sums, "y", None)
    sums = sums + jnp.roll(over(sums, "z", 8, 4), -4, 2)
    got = [sums] + [jnp.roll(over(sums, "z", 8, s), -s, 2) for s in (1, 2, 3)]
    sums = (got[0] + got[2]) + (got[1] + got[3])

    terms = jnp.sum(jnp.log(sums[0]) - sums[1], 2)
    terms = (terms[0] + terms[2]) + (terms[1] + terms[3])
    terms = terms[:4] + terms[4:]
    terms = (terms[0] + terms[2]) + (terms[1] + terms[3])
    loss = (terms + lax.ppermute(terms, "c", swap)) / (64 * rows)

    totals = sums[0].reshape(1, tokens)
    factor = 1.0 - (capped / soft_ceiling) ** 2
    grad = ((exponent / totals - matches.astype(f32)) * factor).astype(bf16)

    both = jnp.stack([jnp.stack([quarter_at(quarters, -s), quarter_at(beside, -s)]) for s in range(4)])
    both = both.reshape(2 * entries, width)
    per = tokens // 4
    whole, sent = {}, []
    for a in (2, 1, 3, 0):
        piece = grad[:, a * per : (a + 1) * per]
        whole[a] = jnp.concatenate([piece] + [over(piece, "y", 4, s) for s in (1, 2, 3)], 0)
        part = lax.dot_general(whole[a], both, (((0,), (0,)), ((), ())), preferred_element_type=f32)
        sent.append(over(part, "x", 4, a) if a else part)
    part = (sent[0] + sent[3]) + (sent[1] + sent[2])
    part = part.reshape(8, rows, width)
    hidden_grad = part[0]
    for b in range(1, 8):
        hidden_grad = hidden_grad + over(part[b].astype(bf16), "z", 8, b).astype(f32)

    all_grad = jnp.concatenate([whole[a] for a in range(4)], 1).reshape(4, 2, quarter, tokens)
    all_grad = jnp.concatenate([all_grad[:, 0], lax.ppermute(all_grad[:, 1], "c", swap)], 2)
    all_grad = jnp.take(all_grad, (y - jnp.arange(4)) % 4, axis=0).reshape(entries, 2 * tokens)
    states2 = jnp.concatenate([own_states, beside_states], 0)
    table_grad = jnp.dot(all_grad, states2, preferred_element_type=f32)
    return (loss, hidden_grad, table_grad)


def solution(mesh):
    cut = Mesh(mesh.devices.reshape(8, 4, 2, 4), ("z", "x", "c", "y"))
    vocab = ("z", "x", "c")
    placed = (P(vocab, "y"), P(vocab, "y"), P(vocab))
    return jax.shard_map(
        local,
        mesh=cut,
        in_specs=placed,
        out_specs=(P(), P(vocab, "y"), P(vocab, "y")),
        check_vma=False,
    )
```

```python
import functools

import jax
import jax.numpy as jnp
from jax import lax
from jax.experimental import pallas as pl
from jax.experimental.pallas import tpu as pltpu
from jax.sharding import Mesh, PartitionSpec as P

soft_ceiling = 30.0
swap = [(0, 1), (1, 0)]
f32, bf16 = jnp.float32, jnp.bfloat16
VM = pltpu.VMEM
NT = (((1,), (1,)), ((), ()))
order = (2, 1, 3, 0)


def over(value, axis, n, s):
    return lax.ppermute(value, axis, [(i, (i + s) % n) for i in range(n)])


def beside_of(value):
    return lax.ppermute(value, "c", swap)


def tie(*values):
    return lax.optimization_barrier(values)


def limit(mib=48):
    return pltpu.CompilerParams(vmem_limit_bytes=mib << 20)


def logits_kernel(h_at, e_at, pos, *refs):
    n_in = len(h_at) + len(e_at[0]) + len(e_at[1])
    ins, (capped_ref, sums_ref, wanted_ref, states, table, sems) = refs[:n_in], refs[n_in:]
    quarter, width = table.shape[2:]
    tokens = states.shape[0]
    full = 4 * width
    copies = []

    def bring(src, dst):
        copy = pltpu.make_async_copy(src, dst, sems.at[len(copies)])
        copies.append(copy)
        copy.start()

    for ref, places in zip(ins, h_at):
        for k, (row, size, col, cols) in enumerate(places):
            src = ref.at[pl.ds(k * size, size)]
            bring(src, states.at[pl.ds(row, size), pl.ds(col, cols)])
    n_states = len(copies)
    ends = []
    i = len(h_at)
    for half in range(2):
        for s, row, size in e_at[half]:
            bring(ins[i], table.at[half, s, pl.ds(row, size)])
            i += 1
        ends.append(len(copies))
    for copy in copies[:n_states]:
        copy.wait()

    lane = lax.broadcasted_iota(jnp.int32, (8, 128), 1)
    row8 = lax.broadcasted_iota(jnp.int32, (8, 128), 0)
    scale = jnp.where(lane == 0, 1.0, jnp.where(lane == 1, 256.0, jnp.where(lane == 2, 65536.0, 0.0)))
    scale = scale.astype(bf16)
    wanted = lax.dot_general(scale, states[:, full:], NT, preferred_element_type=f32)[:1].astype(jnp.int32)
    wanted_ref[...] = wanted
    total = jnp.zeros((1, tokens), f32)
    chosen = jnp.zeros((1, tokens), f32)
    tile = 256
    for half in range(2):
        for copy in copies[ends[half - 1] if half else n_states : ends[half]]:
            copy.wait()
        for t in range(quarter // tile):
            rows = pl.ds(t * tile, tile)
            logits = None
            for s in range(4):
                term = lax.dot_general(
                    table[half, s, rows], states[:, s * width : (s + 1) * width], NT, preferred_element_type=f32
                )
                logits = term if logits is None else logits + term
            capped = soft_ceiling * jnp.tanh(logits / soft_ceiling)
            capped_ref[pl.ds(half * quarter + t * tile, tile), :] = capped
            total = total + jnp.sum(jnp.exp(capped), 0, keepdims=True)
            ids = pos[4 + half] + t * tile + lax.broadcasted_iota(jnp.int32, (tile, tokens), 0)
            chosen = chosen + jnp.sum(jnp.where(ids == wanted, capped, 0.0), 0, keepdims=True)
    per = tokens // 4
    sums = [v[:, a * per : (a + 1) * per] for v in (total, chosen) for a in range(4)]
    sums = jnp.concatenate(sums, 0)
    x, z = pos[0], pos[2]
    sums = jnp.where(row8 % 4 >= x, pltpu.roll(sums, x, 0), pltpu.roll(sums, lax.rem(x + 4, 8), 0))
    sums_ref[...] = pltpu.roll(sums, z * 16, 1)


def logits_of(pos, h_pieces, h_at, e_pieces, e_at, tokens, width, quarter):
    n = sum(len(p) for p in h_at) + len(e_at[0]) + len(e_at[1])
    lanes = 4 * width + 128
    return pl.pallas_call(
        functools.partial(logits_kernel, h_at, e_at),
        out_shape=(
            jax.ShapeDtypeStruct((2 * quarter, tokens), f32),
            jax.ShapeDtypeStruct((8, 128), f32),
            jax.ShapeDtypeStruct((1, tokens), jnp.int32),
        ),
        in_specs=[pl.BlockSpec(memory_space=pltpu.SMEM)]
        + [pl.BlockSpec(memory_space=pl.ANY)] * (len(h_pieces) + len(e_pieces)),
        out_specs=tuple(pl.BlockSpec(memory_space=VM) for _ in range(3)),
        scratch_shapes=[
            VM((tokens, lanes), bf16),
            VM((2, 4, quarter, width), bf16),
            pltpu.SemaphoreType.DMA((n,)),
        ],
        compiler_params=limit(),
        cost_estimate=pl.CostEstimate(
            flops=2 * 2 * quarter * tokens * 4 * width, bytes_accessed=13 << 20, transcendentals=4 * quarter * tokens
        ),
    )(pos, *h_pieces, *e_pieces)


def grad_kernel(pos, q0, q1, q2, q3, capped_ref, wanted_ref, sums_ref, *outs):
    sums = (q0[...] + q2[...]) + (q1[...] + q3[...])
    sums_ref[...] = sums
    x, z = pos[0], pos[2]
    row8 = lax.broadcasted_iota(jnp.int32, (8, 128), 0)
    sums = pltpu.roll(sums, lax.rem(128 - z * 16, 128), 1)
    sums = jnp.where(row8 % 4 + x < 4, pltpu.roll(sums, lax.rem(8 - x, 8), 0), pltpu.roll(sums, 4 - x, 0))
    entries, per = outs[0].shape
    tile = 128
    half = entries // 2
    for a in range(4):
        lanes = slice(a * per, (a + 1) * per)
        totals = sums[a : a + 1]
        wanted = wanted_ref[:, lanes]

        @pl.loop(0, entries // tile)
        def _(i):
            capped = capped_ref[pl.ds(pl.multiple_of(i * tile, tile), tile), lanes]
            first = jnp.where(i * tile < half, pos[4], pos[5] - half) + i * tile
            ids = first + lax.broadcasted_iota(jnp.int32, (tile, per), 0)
            ratio = capped / soft_ceiling
            share = jnp.exp(capped) / totals - jnp.where(ids == wanted, 1.0, 0.0)
            outs[a][pl.ds(pl.multiple_of(i * tile, tile), tile), :] = (share * (1.0 - ratio * ratio)).astype(bf16)


def grad_of(pos, got, capped, wanted):
    entries, tokens = capped.shape
    return pl.pallas_call(
        grad_kernel,
        out_shape=(jax.ShapeDtypeStruct((8, 128), f32),)
        + tuple(jax.ShapeDtypeStruct((entries, tokens // 4), bf16) for _ in range(4)),
        in_specs=[pl.BlockSpec(memory_space=pltpu.SMEM)] + [pl.BlockSpec(memory_space=VM)] * 6,
        out_specs=tuple(pl.BlockSpec(memory_space=VM) for _ in range(5)),
        compiler_params=limit(),
        cost_estimate=pl.CostEstimate(flops=8 * entries * tokens, bytes_accessed=3 << 20, transcendentals=entries * tokens),
    )(pos, *got, capped, wanted)


def table_kernel(pos, own_states, beside_states, *refs):
    ins, (out, grads, states, result, sems) = refs[:20], refs[20:]
    tokens, width = own_states.shape
    quarter = grads.shape[0]
    per = tokens // 4
    states[:tokens] = own_states[...]
    states[tokens:] = beside_states[...]
    copies = [None, None]
    tile = 256
    for s in range(4):
        for a in range(4):
            grads[:, a * per : (a + 1) * per] = ins[4 * s + a][:quarter]
            lanes = slice(tokens + a * per, tokens + (a + 1) * per)
            grads[:, lanes] = ins[16 + a][s * quarter : (s + 1) * quarter]
        slot = s % 2
        if copies[slot] is not None:
            copies[slot].wait()

        @pl.loop(0, quarter // tile)
        def _(i):
            rows = pl.ds(pl.multiple_of(i * tile, tile), tile)
            result[slot, rows, :] = jnp.dot(grads[rows, :], states[...], preferred_element_type=f32)

        at = pl.multiple_of(lax.rem(pos[1] + 4 - s, 4) * quarter, quarter)
        copies[slot] = pltpu.make_async_copy(result.at[slot], out.at[pl.ds(at, quarter)], sems.at[slot])
        copies[slot].start()
    for copy in copies:
        copy.wait()


def table_grad_of(pos, own_states, beside_states, pieces, entries):
    tokens, width = own_states.shape
    quarter = entries // 4
    return pl.pallas_call(
        table_kernel,
        out_shape=jax.ShapeDtypeStruct((entries, width), f32),
        in_specs=[pl.BlockSpec(memory_space=pltpu.SMEM)] + [pl.BlockSpec(memory_space=VM)] * (2 + len(pieces)),
        out_specs=pl.BlockSpec(memory_space=pl.ANY),
        scratch_shapes=[
            VM((quarter, 2 * tokens), bf16),
            VM((2 * tokens, width), bf16),
            VM((2, quarter, width), f32),
            pltpu.SemaphoreType.DMA((2,)),
        ],
        compiler_params=limit(),
        cost_estimate=pl.CostEstimate(flops=4 * entries * tokens * width, bytes_accessed=14 << 20, transcendentals=0),
    )(pos, own_states, beside_states, *pieces)


def local(hidden_states, embedding, targets):
    z, x, c, y = (lax.axis_index(a) for a in ("z", "x", "c", "y"))
    rows, width = hidden_states.shape
    entries = embedding.shape[0]
    quarter = entries // 4
    tokens = 32 * rows
    chip = (z * 4 + x) * 2
    first = [(chip + c) * entries + y * quarter, (chip + 1 - c) * entries + y * quarter]
    pos = jnp.stack([x, y, z, c] + first).astype(jnp.int32)

    parts = [hidden_states] + [over(hidden_states, "y", 4, s) for s in (1, 2, 3)]
    digits = jnp.stack([targets & 255, (targets >> 8) & 255, targets >> 16], 1).astype(bf16)
    digits = jnp.pad(digits, ((0, 0), (0, 125)))
    block_a = jnp.concatenate(parts[:2], 1)
    block_b = jnp.concatenate(parts[2:] + [digits], 1)

    quarters = embedding.reshape(4, quarter, width)

    def quarter_at(q, k):
        return lax.dynamic_index_in_dim(q, (y + k) % 4, 0, False)

    own = [quarter_at(quarters, 0)] + [quarter_at(quarters, s) for s in (1, 2, 3)]
    own[1] = over(own[1], "y", 4, 1)
    own[3] = over(own[3], "y", 4, 3)
    beside = beside_of(embedding).reshape(4, quarter, width)

    at_x = jnp.stack([block_a] + [over(block_a, "x", 4, -a) for a in (1, 2, 3)])
    at_z = jnp.stack([block_b] + [over(block_b, "z", 8, -b) for b in range(1, 8)])
    at_z = at_z.reshape(8 * rows, -1)
    by_x = [at_z] + [over(at_z, "x", 4, -a) for a in (1, 2, 3)]
    up, down = [at_x], [at_x]
    up.append(over(at_x, "z", 8, -1))
    down.append(over(at_x, "z", 8, 1))
    up[1], down[1], own[1], own[3] = tie(up[1], down[1], own[1], own[3])
    send = tie(own[2], own[1])
    half = quarter // 2
    own_2a = over(send[0][:half], "y", 4, 2)
    own_2b = over(send[0][half:], "y", 4, 2)
    up.append(over(up[1], "z", 8, -1))
    down.append(over(down[1], "z", 8, 1))
    up.append(over(up[2], "z", 8, -1))
    down.append(over(down[2], "z", 8, 1))
    up[3], down[3], own_2a = tie(up[3], down[3], own_2a)
    far = [over(up[3][:2], "z", 8, -1), over(down[3][2:], "z", 8, 1)]

    wide_a = block_a.shape[1]
    wide_b = block_b.shape[1]
    h_pieces, h_at = [], []
    for b, piece in enumerate([at_x, up[1], up[2], up[3], None, down[3], down[2], down[1]]):
        if piece is None:
            for k in range(2):
                h_pieces.append(far[k].reshape(2 * rows, wide_a))
                h_at.append([((2 * k + a) * 8 * rows + b * rows, rows, 0, wide_a) for a in range(2)])
        else:
            h_pieces.append(piece.reshape(4 * rows, wide_a))
            h_at.append([(a * 8 * rows + b * rows, rows, 0, wide_a) for a in range(4)])
    for a in range(4):
        h_pieces.append(by_x[a])
        h_at.append([(a * 8 * rows, 8 * rows, wide_a, wide_b)])

    own_pieces = [own[0], own[1], own[3], own_2a, own_2b]
    other_pieces = [quarter_at(beside, 0)] + [beside_of(p) for p in own_pieces[1:]]
    at = [(0, 0, quarter), (1, 0, quarter), (3, 0, quarter), (2, 0, half), (2, half, half)]
    capped, sums, wanted = logits_of(
        pos, h_pieces, h_at, own_pieces + other_pieces, (at, at), tokens, width, quarter
    )

    own_states = jnp.stack([p.reshape(-1, rows, wide_a)[:, :, :width] for p in (at_x, *up[1:])], 1)
    far_states = jnp.concatenate([far[0], far[1]], 0)[:, :, :width]
    down_states = jnp.stack([down[k][:, :, :width] for k in (3, 2, 1)], 1)
    own_states = jnp.concatenate([own_states, far_states[:, None], down_states], 1).reshape(tokens, width)
    beside_states = beside_of(own_states)

    got = [sums] + [over(sums, "x", 4, s) for s in (1, 2, 3)]
    sums = (got[0] + got[2]) + (got[1] + got[3])
    got = [sums] + [over(sums, "y", 4, s) for s in (1, 2, 3)]
    sums = (got[0] + got[2]) + (got[1] + got[3])
    sums = sums + over(sums, "z", 8, 4)
    got = [sums] + [over(sums, "z", 8, s) for s in (1, 2, 3)]
    sums, *grad = grad_of(pos, got, capped, wanted)

    terms = jnp.sum(jnp.log(sums[:4]) - sums[4:])
    loss = (terms + beside_of(terms)) / (2 * tokens)

    embedding_late, beside_late, capped = tie(embedding, beside, capped)
    quarters = embedding_late.reshape(4, quarter, width)
    both = [(quarter_at(quarters, -s), quarter_at(beside_late, -s)) for s in range(4)]

    def back(piece, rows_of):
        return lax.dot_general(piece, rows_of, (((0,), (0,)), ((), ())), preferred_element_type=f32)

    near, after, parts, lower = {}, {}, {}, {}

    def first_hop(a):
        near[a] = (over(grad[a], "y", 4, 1), over(grad[a], "y", 4, 3))

    first_hop(order[0])
    for i, a in enumerate(order):
        if i < 3:
            first_hop(order[i + 1])
        plus, minus = near[a]
        if i > 0:
            plus, minus, parts[order[i - 1]] = tie(plus, minus, parts[order[i - 1]])
            near[a] = plus, minus
        if i > 0:
            b = order[i - 1]
            parts[b] = over(parts[b], "x", 4, b)
        after[a] = (over(plus[:quarter], "y", 4, 1), over(minus[quarter:], "y", 4, 3))
        part = None
        for s, g in ((0, grad[a]), (1, plus), (3, minus)):
            for k in range(2):
                term = back(g[k * quarter : (k + 1) * quarter], both[s][k])
                part = term if part is None else part + term
        parts[a] = part + back(after[a][0], both[2][0]) + back(after[a][1], both[2][1])
        lower[a] = beside_of(
            jnp.concatenate([grad[a][quarter:], plus[quarter:], after[a][1], minus[quarter:]], 0)
        )
    part = (parts[0] + parts[2]) + (parts[1] + parts[3])
    part = part.reshape(8, rows, width)
    hidden_grad = part[0]
    for b in range(1, 8):
        hidden_grad = hidden_grad + over(part[b].astype(bf16), "z", 8, b).astype(f32)

    pieces = grad + [near[a][0] for a in range(4)] + [after[a][0] for a in range(4)] + [near[a][1] for a in range(4)]
    table_grad = table_grad_of(pos, own_states, beside_states, pieces + [lower[a] for a in range(4)], entries)
    return (loss, hidden_grad, table_grad)


def solution(mesh):
    cut = Mesh(mesh.devices.reshape(8, 4, 2, 4), ("z", "x", "c", "y"))
    vocab = ("z", "x", "c")
    placed = (P(vocab, "y"), P(vocab, "y"), P(vocab))
    return jax.shard_map(
        local,
        mesh=cut,
        in_specs=placed,
        out_specs=(P(), P(vocab, "y"), P(vocab, "y")),
        check_vma=False,
    )
```

```python
import functools

import jax
import jax.numpy as jnp
from jax import lax
from jax.experimental import pallas as pl
from jax.experimental.pallas import tpu as pltpu
from jax.sharding import Mesh, PartitionSpec as P

soft_ceiling = 30.0
swap = [(0, 1), (1, 0)]
f32, bf16 = jnp.float32, jnp.bfloat16
VM = pltpu.VMEM
NT = (((1,), (1,)), ((), ()))

def over(value, axis, n, s):
    return lax.ppermute(value, axis, [(i, (i + s) % n) for i in range(n)])


def beside_of(value):
    return lax.ppermute(value, "c", swap)


def tie(*values):
    return lax.optimization_barrier(values)


def in_hbm(*values):
    return [pltpu.with_memory_space_constraint(v, pltpu.HBM) for v in values]


def limit(mib):
    return pltpu.CompilerParams(vmem_limit_bytes=mib << 20)


def logits_kernel(pos, *refs):
    rows_ref, *ins = refs[:9]
    capped_ref, sums_ref, wanted_ref, own_ref, states, table, held, sems, out_sems = refs[9:]
    quarter, full = table.shape[1:]
    width = full // 4
    tokens = states.shape[0]
    copies = []

    def bring(src, dst):
        copy = pltpu.make_async_copy(src, dst, sems.at[len(copies)])
        copies.append(copy)
        copy.start()

    y = pos[1]
    size = tokens // 16
    for h in range(2):
        for z in range(8):
            bring(rows_ref.at[pl.ds((2 * z + h) * size, size)], states.at[pl.ds((8 * h + z) * size, size)])
    n_states = len(copies)
    ends = []
    for half in range(2):
        quarters, *arrived = ins[4 * half : 4 * half + 4]
        for s, src in enumerate([quarters.at[y], *arrived]):
            lanes = pl.ds(pl.multiple_of(lax.rem(y + 4 - s, 4) * width, width), width)
            bring(src, table.at[half, :, lanes])
        ends.append(len(copies))
    for copy in copies[:n_states]:
        copy.wait()

    lane = lax.broadcasted_iota(jnp.int32, (8, 128), 1)
    scale = jnp.where(lane == 0, 1.0, jnp.where(lane == 1, 256.0, jnp.where(lane == 2, 65536.0, 0.0)))
    scale = scale.astype(bf16)
    wanted = lax.dot_general(scale, states[:, full:], NT, preferred_element_type=f32)[:1].astype(jnp.int32)
    wanted_ref[...] = wanted
    total = jnp.zeros((1, tokens), f32)
    chosen = jnp.zeros((1, tokens), f32)
    tile = held.shape[1]
    outs = [pltpu.make_async_copy(states.at[:, pl.ds(pl.multiple_of(y * width, width), width)], own_ref, out_sems.at[held.shape[0]])]
    outs[0].start()
    for half in range(2):
        for copy in copies[ends[half - 1] if half else n_states : ends[half]]:
            copy.wait()
        for t in range(quarter // tile):
            rows = pl.ds(t * tile, tile)
            logits = lax.dot_general(table[half, rows], states[:, :full], NT, preferred_element_type=f32)
            capped = soft_ceiling * jnp.tanh(logits / soft_ceiling)
            k = half * (quarter // tile) + t
            held[k] = capped
            outs.append(pltpu.make_async_copy(held.at[k], capped_ref.at[pl.ds(k * tile, tile)], out_sems.at[k]))
            outs[-1].start()
            total = total + jnp.sum(jnp.exp(capped), 0, keepdims=True)
            ids = pos[4 + half] + t * tile + lax.broadcasted_iota(jnp.int32, (tile, tokens), 0)
            chosen = chosen + jnp.sum(jnp.where(ids == wanted, capped, 0.0), 0, keepdims=True)
    per = tokens // 4
    sums = [v[:, a * per : (a + 1) * per] for v in (total, chosen) for a in range(4)]
    sums_ref[...] = jnp.concatenate(sums, 0)
    for out in outs:
        out.wait()


def logits_of(pos, token_rows, entry_pieces, width, quarter):
    tokens = token_rows.shape[0]
    tile = 512
    lanes = 4 * width + 128
    return pl.pallas_call(
        logits_kernel,
        out_shape=(
            jax.ShapeDtypeStruct((2 * quarter, tokens), f32),
            jax.ShapeDtypeStruct((8, 128), f32),
            jax.ShapeDtypeStruct((1, tokens), jnp.int32),
            jax.ShapeDtypeStruct((tokens, width), bf16),
        ),
        in_specs=[pl.BlockSpec(memory_space=pltpu.SMEM)]
        + [pl.BlockSpec(memory_space=pltpu.HBM)] * (1 + len(entry_pieces)),
        out_specs=(
            pl.BlockSpec(memory_space=pltpu.HBM),
            pl.BlockSpec(memory_space=VM),
            pl.BlockSpec(memory_space=VM),
            pl.BlockSpec(memory_space=pltpu.HBM),
        ),
        scratch_shapes=[
            VM((tokens, lanes), bf16),
            VM((2, quarter, 4 * width), bf16),
            VM((2 * quarter // tile, tile, tokens), f32),
            pltpu.SemaphoreType.DMA((24,)),
            pltpu.SemaphoreType.DMA((2 * quarter // tile + 1,)),
        ],
        compiler_params=limit(26),
        cost_estimate=pl.CostEstimate(
            flops=2 * 2 * quarter * tokens * 4 * width, bytes_accessed=13 << 20, transcendentals=4 * quarter * tokens
        ),
    )(pos, *in_hbm(token_rows, *entry_pieces))


def logit_grad(capped, totals, ids, wanted):
    ratio = capped / soft_ceiling
    share = jnp.exp(capped) / totals - jnp.where(ids == wanted, 1.0, 0.0)
    return (share * (1.0 - ratio * ratio)).astype(bf16)


def grad_kernel(half, pos, got, capped_ref, wanted_ref, sums_ref, *outs):
    sums = got[0]
    for k in range(1, got.shape[0]):
        sums = sums + got[k]
    sums_ref[...] = sums
    tile, wide = capped_ref.shape
    start = pl.program_id(0) * tile
    first = jnp.where(start < half, pos[4], pos[5] - half) + start
    ids = first + lax.broadcasted_iota(jnp.int32, (tile, 128), 0)
    for at in range(0, wide, 128):
        row = at // 128
        wanted = wanted_ref[:, at : at + 128]
        out = outs[2 * at // wide]
        put = at % (wide // 2)
        out[:, put : put + 128] = logit_grad(capped_ref[:, at : at + 128], sums[row : row + 1], ids, wanted)


def grad_of(pos, got, capped, wanted):
    entries, wide = capped.shape
    tile = entries // 4
    return pl.pallas_call(
        functools.partial(grad_kernel, entries // 2),
        grid=(entries // tile,),
        out_shape=(jax.ShapeDtypeStruct((8, 128), f32),) + (jax.ShapeDtypeStruct((entries, wide // 2), bf16),) * 2,
        in_specs=[
            pl.BlockSpec(memory_space=pltpu.SMEM),
            pl.BlockSpec(got.shape, lambda i: (0, 0, 0)),
            pl.BlockSpec((tile, wide), lambda i: (i, 0)),
            pl.BlockSpec(wanted.shape, lambda i: (0, 0)),
        ],
        out_specs=(pl.BlockSpec((8, 128), lambda i: (0, 0)),) + (pl.BlockSpec((tile, wide // 2), lambda i: (i, 0)),) * 2,
        compiler_params=limit(12),
        cost_estimate=pl.CostEstimate(flops=8 * entries * wide, bytes_accessed=3 << 20, transcendentals=entries * wide),
    )(pos, got, *in_hbm(capped), wanted)


def pack_kernel(*refs):
    ins, out, sems = refs[:-2], refs[-2], refs[-1]
    half = ins[0].shape[0] // 2
    copies = []
    for s, ref in enumerate(ins):
        copies.append(pltpu.make_async_copy(ref.at[pl.ds(half, half)], out.at[pl.ds(s * half, half)], sems.at[s]))
        copies[-1].start()
    for copy in copies:
        copy.wait()


def lower_halves(pieces):
    rows, wide = pieces[0].shape
    return pl.pallas_call(
        pack_kernel,
        out_shape=jax.ShapeDtypeStruct((len(pieces) * rows // 2, wide), bf16),
        in_specs=[pl.BlockSpec(memory_space=pltpu.HBM)] * len(pieces),
        out_specs=pl.BlockSpec(memory_space=pltpu.HBM),
        scratch_shapes=[pltpu.SemaphoreType.DMA((len(pieces),))],
        compiler_params=limit(1),
        cost_estimate=pl.CostEstimate(flops=0, bytes_accessed=1 << 16, transcendentals=0),
    )(*in_hbm(*pieces))


def table_kernel(pos, own_states, beside_states, *refs):
    moved, lower, (out, grads, states, result, sems, out_sems) = refs[:8], refs[8:10], refs[10:]
    tokens, width = own_states.shape
    quarter = grads.shape[1]
    copies = []

    def bring(src, dst):
        copy = pltpu.make_async_copy(src, dst, sems.at[len(copies)])
        copies.append(copy)
        copy.start()

    bring(own_states, states.at[pl.ds(0, tokens)])
    bring(beside_states, states.at[pl.ds(tokens, tokens)])
    for s in range(4):
        for h in range(2):
            wide = tokens // 2
            bring(moved[4 * h + s].at[pl.ds(0, quarter)], grads.at[s, :, pl.ds(h * wide, wide)])
            bring(lower[h].at[pl.ds(s * quarter, quarter)], grads.at[s, :, pl.ds(tokens + h * wide, wide)])
    for copy in copies[:2]:
        copy.wait()
    outs = [None, None]
    tile = 256
    for s in range(4):
        for copy in copies[2 + 4 * s : 6 + 4 * s]:
            copy.wait()
        slot = s % 2
        if outs[slot] is not None:
            outs[slot].wait()

        @pl.loop(0, quarter // tile)
        def _(i):
            rows = pl.ds(pl.multiple_of(i * tile, tile), tile)
            result[slot, rows, :] = jnp.dot(grads[s, rows, :], states[...], preferred_element_type=f32)

        at = pl.multiple_of(lax.rem(pos[1] + 4 - s, 4) * quarter, quarter)
        outs[slot] = pltpu.make_async_copy(result.at[slot], out.at[pl.ds(at, quarter)], out_sems.at[slot])
        outs[slot].start()
    for copy in outs:
        copy.wait()


def table_grad_of(pos, own_states, beside_states, pieces, entries):
    tokens, width = own_states.shape
    quarter = entries // 4
    return pl.pallas_call(
        table_kernel,
        out_shape=jax.ShapeDtypeStruct((entries, width), f32),
        in_specs=[pl.BlockSpec(memory_space=pltpu.SMEM)] + [pl.BlockSpec(memory_space=pltpu.HBM)] * (2 + len(pieces)),
        out_specs=pl.BlockSpec(memory_space=pltpu.HBM),
        scratch_shapes=[
            VM((4, quarter, 2 * tokens), bf16),
            VM((2 * tokens, width), bf16),
            VM((2, quarter, width), f32),
            pltpu.SemaphoreType.DMA((18,)),
            pltpu.SemaphoreType.DMA((2,)),
        ],
        compiler_params=limit(20),
        cost_estimate=pl.CostEstimate(flops=1 << 20, bytes_accessed=1 << 18, transcendentals=0),
    )(pos, *in_hbm(own_states, beside_states, *pieces))


def local(hidden_states, embedding, targets):
    z, x, c, y = (lax.axis_index(a) for a in ("z", "x", "c", "y"))
    rows, width = hidden_states.shape
    entries = embedding.shape[0]
    quarter = entries // 4
    tokens = 32 * rows
    chip = (z * 4 + x) * 2
    first = [(chip + c) * entries + y * quarter, (chip + 1 - c) * entries + y * quarter]
    pos = jnp.stack([x, y, z, c, *first]).astype(jnp.int32)

    digits = jnp.stack([targets & 255, (targets >> 8) & 255, targets >> 16], 1).astype(bf16)
    block = jnp.concatenate([hidden_states, jnp.pad(digits, ((0, 0), (0, 125)))], 1)
    got = lax.all_to_all(jnp.broadcast_to(block, (16, *block.shape)), ("x", "y"), 0, 0, tiled=True)

    quarters = embedding.reshape(4, quarter, width)
    beside = beside_of(embedding).reshape(4, quarter, width)

    def quarter_at(q, k):
        return lax.dynamic_index_in_dim(q, (y + k) % 4, 0, False)

    own = {s: over(quarter_at(quarters, s), "y", 4, s) for s in (1, 3, 2)}
    other = {s: beside_of(own[s]) for s in (1, 3, 2)}

    got = got.reshape(4, 4, 2, rows // 2, width + 128).transpose(2, 0, 1, 3, 4)
    at_x = jnp.concatenate([got[:, :, k, :, :width] for k in range(4)] + [got[:, :, 0, :, width:]], 3)
    token_rows = lax.all_gather(at_x.reshape(4 * rows, -1), "z", axis=0, tiled=True)

    entry_pieces = (quarters, own[1], own[2], own[3], beside, other[1], other[2], other[3])
    capped, sums, wanted, own_states = logits_of(pos, token_rows, entry_pieces, width, quarter)

    got = lax.all_to_all(jnp.broadcast_to(sums, (16, *sums.shape)), ("x", "y"), 0, 0, tiled=True)
    sums = jnp.sum(got, 0)
    got = lax.all_to_all(jnp.broadcast_to(sums, (8, *sums.shape)), "z", 0, 0, tiled=True)
    sums, *grad = grad_of(pos, got, capped, wanted)
    beside_states = beside_of(own_states)
    moved = [[g] + [over(g, "y", 4, s) for s in (1, 2, 3)] for g in grad]

    def back(pieces):
        part = None
        for s in (0, 1, 3, 2):
            term = lax.dot_general(pieces[s], both[s], (((0,), (0,)), ((), ())), preferred_element_type=f32)
            part = term if part is None else part + term
        return part.astype(bf16).reshape(32, rows // 2, width)

    late, beside_late, moved[0][0] = tie(quarters, beside, moved[0][0])
    both = [jnp.concatenate([quarter_at(late, -s), quarter_at(beside_late, -s)]) for s in range(4)]
    home = back(moved[0])
    moved[1][2], home = tie(moved[1][2], home)
    got = [lax.all_to_all(home, ("z", "x"), 0, 0, tiled=True)]
    home = back(moved[1])
    got.append(lax.all_to_all(home, ("z", "x"), 0, 0, tiled=True))
    lower = [beside_of(lower_halves(pieces)) for pieces in moved]
    table_grad = table_grad_of(pos, own_states, beside_states, [*moved[0], *moved[1], *lower], entries)
    got[1], table_grad = tie(got[1], table_grad)
    hidden_grad = jnp.concatenate([jnp.sum(v.astype(f32), 0) for v in got], 0)

    terms = jnp.sum(jnp.log(sums[:4]) - sums[4:])
    loss = (terms + beside_of(terms)) / (2 * tokens)

    return (loss, hidden_grad, table_grad)


def solution(mesh):
    cut = Mesh(mesh.devices.reshape(8, 4, 2, 4), ("z", "x", "c", "y"))
    vocab = ("z", "x", "c")
    placed = (P(vocab, "y"), P(vocab, "y"), P(vocab))
    return jax.shard_map(
        local,
        mesh=cut,
        in_specs=placed,
        out_specs=(P(), P(vocab, "y"), P(vocab, "y")),
        check_vma=False,
    )
```

```python
import functools

import jax
import jax.numpy as jnp
from jax import lax
from jax.experimental import pallas as pl
from jax.experimental.pallas import tpu as pltpu
from jax.sharding import Mesh, PartitionSpec as P

soft_ceiling = 30.0
swap = [(0, 1), (1, 0)]
f32, bf16 = jnp.float32, jnp.bfloat16
VM = pltpu.VMEM
NT = (((1,), (1,)), ((), ()))

def over(value, axis, n, s):
    return lax.ppermute(value, axis, [(i, (i + s) % n) for i in range(n)])


def beside_of(value):
    return lax.ppermute(value, "c", swap)


def tie(*values):
    return lax.optimization_barrier(values)


def in_hbm(*values):
    return [pltpu.with_memory_space_constraint(v, pltpu.HBM) for v in values]


def limit(mib):
    return pltpu.CompilerParams(vmem_limit_bytes=mib << 20)


def logits_kernel(pos, *refs):
    pieces, ins = refs[:9], refs[9:17]
    capped_ref, sums_ref, wanted_ref, own_ref, states, table, held, sems, out_sems = refs[17:]
    quarter, full = table.shape[1:]
    width = full // 4
    tokens = states.shape[0]
    copies = []

    def bring(src, dst):
        copy = pltpu.make_async_copy(src, dst, sems.at[len(copies)])
        copies.append(copy)
        copy.start()

    y = pos[1]
    size = tokens // 16
    for b in range(8):
        place = lax.rem(pos[2] + b, 8)
        for h in range(2):
            src = pieces[4 + h] if b == 4 else pieces[b if b < 4 else b + 1].at[h]
            row = pl.multiple_of((8 * h + place) * size, size)
            bring(src, states.at[pl.ds(row, size)])
    n_states = len(copies)
    ends = []
    for half in range(2):
        quarters, *arrived = ins[4 * half : 4 * half + 4]
        for s, src in enumerate([quarters.at[y], *arrived]):
            lanes = pl.ds(pl.multiple_of(lax.rem(y + 4 - s, 4) * width, width), width)
            bring(src, table.at[half, :, lanes])
        ends.append(len(copies))
    for copy in copies[:n_states]:
        copy.wait()

    lane = lax.broadcasted_iota(jnp.int32, (8, 128), 1)
    scale = jnp.where(lane == 0, 1.0, jnp.where(lane == 1, 256.0, jnp.where(lane == 2, 65536.0, 0.0)))
    scale = scale.astype(bf16)
    wanted = lax.dot_general(scale, states[:, full:], NT, preferred_element_type=f32)[:1].astype(jnp.int32)
    wanted_ref[...] = wanted
    total = jnp.zeros((1, tokens), f32)
    chosen = jnp.zeros((1, tokens), f32)
    tile = held.shape[1]
    outs = [pltpu.make_async_copy(states.at[:, pl.ds(pl.multiple_of(y * width, width), width)], own_ref, out_sems.at[held.shape[0]])]
    outs[0].start()
    for half in range(2):
        for copy in copies[ends[half - 1] if half else n_states : ends[half]]:
            copy.wait()
        for t in range(quarter // tile):
            rows = pl.ds(t * tile, tile)
            logits = lax.dot_general(table[half, rows], states[:, :full], NT, preferred_element_type=f32)
            capped = soft_ceiling * jnp.tanh(logits / soft_ceiling)
            k = half * (quarter // tile) + t
            held[k] = capped
            outs.append(pltpu.make_async_copy(held.at[k], capped_ref.at[pl.ds(k * tile, tile)], out_sems.at[k]))
            outs[-1].start()
            total = total + jnp.sum(jnp.exp(capped), 0, keepdims=True)
            ids = pos[4 + half] + t * tile + lax.broadcasted_iota(jnp.int32, (tile, tokens), 0)
            chosen = chosen + jnp.sum(jnp.where(ids == wanted, capped, 0.0), 0, keepdims=True)
    per = tokens // 4
    sums = [v[:, a * per : (a + 1) * per] for v in (total, chosen) for a in range(4)]
    sums_ref[...] = jnp.concatenate(sums, 0)
    for out in outs:
        out.wait()


def logits_of(pos, row_pieces, entry_pieces, width, quarter):
    tokens = 16 * row_pieces[0].shape[1]
    tile = 512
    lanes = 4 * width + 128
    return pl.pallas_call(
        logits_kernel,
        out_shape=(
            jax.ShapeDtypeStruct((2 * quarter, tokens), f32),
            jax.ShapeDtypeStruct((8, 128), f32),
            jax.ShapeDtypeStruct((1, tokens), jnp.int32),
            jax.ShapeDtypeStruct((tokens, width), bf16),
        ),
        in_specs=[pl.BlockSpec(memory_space=pltpu.SMEM)]
        + [pl.BlockSpec(memory_space=pltpu.HBM)] * (len(row_pieces) + len(entry_pieces)),
        out_specs=(
            pl.BlockSpec(memory_space=pltpu.HBM),
            pl.BlockSpec(memory_space=VM),
            pl.BlockSpec(memory_space=VM),
            pl.BlockSpec(memory_space=pltpu.HBM),
        ),
        scratch_shapes=[
            VM((tokens, lanes), bf16),
            VM((2, quarter, 4 * width), bf16),
            VM((2 * quarter // tile, tile, tokens), f32),
            pltpu.SemaphoreType.DMA((24,)),
            pltpu.SemaphoreType.DMA((2 * quarter // tile + 1,)),
        ],
        compiler_params=limit(26),
        cost_estimate=pl.CostEstimate(
            flops=2 * 2 * quarter * tokens * 4 * width, bytes_accessed=13 << 20, transcendentals=4 * quarter * tokens
        ),
    )(pos, *in_hbm(*row_pieces, *entry_pieces))


def logit_grad(capped, totals, ids, wanted):
    ratio = capped / soft_ceiling
    share = jnp.exp(capped) / totals - jnp.where(ids == wanted, 1.0, 0.0)
    return (share * (1.0 - ratio * ratio)).astype(bf16)


def grad_kernel(half, pos, got, capped_ref, wanted_ref, sums_ref, *outs):
    sums = got[0]
    for k in range(1, got.shape[0]):
        sums = sums + got[k]
    sums_ref[...] = sums
    tile, wide = capped_ref.shape
    start = pl.program_id(0) * tile
    first = jnp.where(start < half, pos[4], pos[5] - half) + start
    ids = first + lax.broadcasted_iota(jnp.int32, (tile, 128), 0)
    for at in range(0, wide, 128):
        row = at // 128
        wanted = wanted_ref[:, at : at + 128]
        out = outs[2 * at // wide]
        put = at % (wide // 2)
        out[:, put : put + 128] = logit_grad(capped_ref[:, at : at + 128], sums[row : row + 1], ids, wanted)


def grad_of(pos, got, capped, wanted):
    entries, wide = capped.shape
    tile = entries // 4
    return pl.pallas_call(
        functools.partial(grad_kernel, entries // 2),
        grid=(entries // tile,),
        out_shape=(jax.ShapeDtypeStruct((8, 128), f32),) + (jax.ShapeDtypeStruct((entries, wide // 2), bf16),) * 2,
        in_specs=[
            pl.BlockSpec(memory_space=pltpu.SMEM),
            pl.BlockSpec(got.shape, lambda i: (0, 0, 0)),
            pl.BlockSpec((tile, wide), lambda i: (i, 0)),
            pl.BlockSpec(wanted.shape, lambda i: (0, 0)),
        ],
        out_specs=(pl.BlockSpec((8, 128), lambda i: (0, 0)),) + (pl.BlockSpec((tile, wide // 2), lambda i: (i, 0)),) * 2,
        compiler_params=limit(12),
        cost_estimate=pl.CostEstimate(flops=8 * entries * wide, bytes_accessed=3 << 20, transcendentals=entries * wide),
    )(pos, got, *in_hbm(capped), wanted)


def pack_kernel(*refs):
    ins, out, sems = refs[:-2], refs[-2], refs[-1]
    half = ins[0].shape[0] // 2
    copies = []
    for s, ref in enumerate(ins):
        copies.append(pltpu.make_async_copy(ref.at[pl.ds(half, half)], out.at[pl.ds(s * half, half)], sems.at[s]))
        copies[-1].start()
    for copy in copies:
        copy.wait()


def lower_halves(pieces):
    rows, wide = pieces[0].shape
    return pl.pallas_call(
        pack_kernel,
        out_shape=jax.ShapeDtypeStruct((len(pieces) * rows // 2, wide), bf16),
        in_specs=[pl.BlockSpec(memory_space=pltpu.HBM)] * len(pieces),
        out_specs=pl.BlockSpec(memory_space=pltpu.HBM),
        scratch_shapes=[pltpu.SemaphoreType.DMA((len(pieces),))],
        compiler_params=limit(1),
        cost_estimate=pl.CostEstimate(flops=0, bytes_accessed=1 << 16, transcendentals=0),
    )(*in_hbm(*pieces))


def table_kernel(pos, own_states, beside_states, *refs):
    moved, lower, (out, grads, states, result, sems, out_sems) = refs[:8], refs[8:10], refs[10:]
    tokens, width = own_states.shape
    quarter = grads.shape[1]
    copies = []

    def bring(src, dst):
        copy = pltpu.make_async_copy(src, dst, sems.at[len(copies)])
        copies.append(copy)
        copy.start()

    bring(own_states, states.at[pl.ds(0, tokens)])
    bring(beside_states, states.at[pl.ds(tokens, tokens)])
    for s in range(4):
        for h in range(2):
            wide = tokens // 2
            bring(moved[4 * h + s].at[pl.ds(0, quarter)], grads.at[s, :, pl.ds(h * wide, wide)])
            bring(lower[h].at[pl.ds(s * quarter, quarter)], grads.at[s, :, pl.ds(tokens + h * wide, wide)])
    for copy in copies[:2]:
        copy.wait()
    outs = [None, None]
    tile = 256
    for s in range(4):
        for copy in copies[2 + 4 * s : 6 + 4 * s]:
            copy.wait()
        slot = s % 2
        if outs[slot] is not None:
            outs[slot].wait()

        @pl.loop(0, quarter // tile)
        def _(i):
            rows = pl.ds(pl.multiple_of(i * tile, tile), tile)
            result[slot, rows, :] = jnp.dot(grads[s, rows, :], states[...], preferred_element_type=f32)

        at = pl.multiple_of(lax.rem(pos[1] + 4 - s, 4) * quarter, quarter)
        outs[slot] = pltpu.make_async_copy(result.at[slot], out.at[pl.ds(at, quarter)], out_sems.at[slot])
        outs[slot].start()
    for copy in outs:
        copy.wait()


def table_grad_of(pos, own_states, beside_states, pieces, entries):
    tokens, width = own_states.shape
    quarter = entries // 4
    return pl.pallas_call(
        table_kernel,
        out_shape=jax.ShapeDtypeStruct((entries, width), f32),
        in_specs=[pl.BlockSpec(memory_space=pltpu.SMEM)] + [pl.BlockSpec(memory_space=pltpu.HBM)] * (2 + len(pieces)),
        out_specs=pl.BlockSpec(memory_space=pltpu.HBM),
        scratch_shapes=[
            VM((4, quarter, 2 * tokens), bf16),
            VM((2 * tokens, width), bf16),
            VM((2, quarter, width), f32),
            pltpu.SemaphoreType.DMA((18,)),
            pltpu.SemaphoreType.DMA((2,)),
        ],
        compiler_params=limit(20),
        cost_estimate=pl.CostEstimate(flops=1 << 20, bytes_accessed=1 << 18, transcendentals=0),
    )(pos, *in_hbm(own_states, beside_states, *pieces))


def local(hidden_states, embedding, targets):
    z, x, c, y = (lax.axis_index(a) for a in ("z", "x", "c", "y"))
    rows, width = hidden_states.shape
    entries = embedding.shape[0]
    quarter = entries // 4
    tokens = 32 * rows
    chip = (z * 4 + x) * 2
    first = [(chip + c) * entries + y * quarter, (chip + 1 - c) * entries + y * quarter]
    pos = jnp.stack([x, y, z, c, *first]).astype(jnp.int32)

    digits = jnp.stack([targets & 255, (targets >> 8) & 255, targets >> 16], 1).astype(bf16)
    block = jnp.concatenate([hidden_states, jnp.pad(digits, ((0, 0), (0, 125)))], 1)
    got = lax.all_to_all(jnp.broadcast_to(block, (16, *block.shape)), ("x", "y"), 0, 0, tiled=True)

    quarters = embedding.reshape(4, quarter, width)
    beside = beside_of(embedding).reshape(4, quarter, width)

    def quarter_at(q, k):
        return lax.dynamic_index_in_dim(q, (y + k) % 4, 0, False)

    own = {s: over(quarter_at(quarters, s), "y", 4, s) for s in (1, 3)}

    got = got.reshape(4, 4, 2, rows // 2, width + 128).transpose(2, 0, 1, 3, 4)
    at_x = jnp.concatenate([got[:, :, k, :, :width] for k in range(4)] + [got[:, :, 0, :, width:]], 3)
    at_x = at_x.reshape(2, 2 * rows, -1)
    up, down = [at_x], [at_x]
    for k in range(3):
        up.append(over(up[-1], "z", 8, -1))
        down.append(over(down[-1], "z", 8, 1))
        if k == 1:
            up[-1], down[-1], own[1], own[3] = tie(up[-1], down[-1], own[1], own[3])
            send, own[1], own[3] = tie(quarter_at(quarters, 2), own[1], own[3])
            own[2] = over(send, "y", 4, 2)
    far = [over(up[3][0], "z", 8, -1), over(down[3][1], "z", 8, 1)]
    own[2], *far = tie(own[2], *far)
    other = {s: beside_of(own[s]) for s in (1, 3, 2)}
    row_pieces = [*up, *far, down[3], down[2], down[1]]

    entry_pieces = (quarters, own[1], own[2], own[3], beside, other[1], other[2], other[3])
    capped, sums, wanted, own_states = logits_of(pos, row_pieces, entry_pieces, width, quarter)

    got = lax.all_to_all(jnp.broadcast_to(sums, (16, *sums.shape)), ("x", "y"), 0, 0, tiled=True)
    sums = jnp.sum(got, 0)
    got = lax.all_to_all(jnp.broadcast_to(sums, (8, *sums.shape)), "z", 0, 0, tiled=True)
    sums, *grad = grad_of(pos, got, capped, wanted)
    beside_states = beside_of(own_states)
    moved = [[grad[0]] + [over(grad[0], "y", 4, s) for s in (1, 2, 3)]]
    grad[1], *moved[0][1:] = tie(grad[1], *moved[0][1:])
    moved.append([grad[1]] + [over(grad[1], "y", 4, s) for s in (1, 2, 3)])

    def back(pieces):
        part = None
        for s in (0, 1, 3, 2):
            term = lax.dot_general(pieces[s], both[s], (((0,), (0,)), ((), ())), preferred_element_type=f32)
            part = term if part is None else part + term
        return part.astype(bf16).reshape(32, rows // 2, width)

    late, beside_late, moved[0][0] = tie(quarters, beside, moved[0][0])
    both = [jnp.concatenate([quarter_at(late, -s), quarter_at(beside_late, -s)]) for s in range(4)]
    home = [back(moved[0])]
    got = [lax.all_to_all(home[0], ("z", "x"), 0, 0, tiled=True)]
    moved[1][2], home[0] = tie(moved[1][2], home[0])
    home.append(back(moved[1]))
    home[1], got[0] = tie(home[1], got[0])
    got.append(lax.all_to_all(home[1], ("z", "x"), 0, 0, tiled=True))
    for k in range(2):
        *moved[k], home[k] = tie(*moved[k], home[k])
    lower = [beside_of(lower_halves(pieces)) for pieces in moved]
    table_grad = table_grad_of(pos, own_states, beside_states, [*moved[0], *moved[1], *lower], entries)
    got[1], table_grad = tie(got[1], table_grad)
    hidden_grad = jnp.concatenate([jnp.sum(v.astype(f32), 0) for v in got], 0)

    terms = jnp.sum(jnp.log(sums[:4]) - sums[4:])
    loss = (terms + beside_of(terms)) / (2 * tokens)

    return (loss, hidden_grad, table_grad)


def solution(mesh):
    cut = Mesh(mesh.devices.reshape(8, 4, 2, 4), ("z", "x", "c", "y"))
    vocab = ("z", "x", "c")
    placed = (P(vocab, "y"), P(vocab, "y"), P(vocab))
    return jax.shard_map(
        local,
        mesh=cut,
        in_specs=placed,
        out_specs=(P(), P(vocab, "y"), P(vocab, "y")),
        check_vma=False,
    )
```

```python
import functools

import jax
import jax.numpy as jnp
from jax import lax
from jax.experimental import pallas as pl
from jax.experimental.pallas import tpu as pltpu
from jax.sharding import Mesh, PartitionSpec as P

soft_ceiling = 30.0
swap = [(0, 1), (1, 0)]
f32, bf16 = jnp.float32, jnp.bfloat16
VM = pltpu.VMEM
NT = (((1,), (1,)), ((), ()))

def over(value, axis, n, s):
    return lax.ppermute(value, axis, [(i, (i + s) % n) for i in range(n)])


def beside_of(value):
    return lax.ppermute(value, "c", swap)


def tie(*values):
    return lax.optimization_barrier(values)


def in_hbm(*values):
    return [pltpu.with_memory_space_constraint(v, pltpu.HBM) for v in values]


def limit(mib):
    return pltpu.CompilerParams(vmem_limit_bytes=mib << 20)


def logits_kernel(pos, *refs):
    pieces, ins = refs[:9], refs[9:17]
    capped_ref, sums_ref, wanted_ref, own_ref, states, table, held, sems, out_sems = refs[17:]
    quarter, full = table.shape[1:]
    width = full // 4
    tokens = states.shape[0]
    copies = []

    def bring(src, dst):
        copy = pltpu.make_async_copy(src, dst, sems.at[len(copies)])
        copies.append(copy)
        copy.start()

    y = pos[1]
    size = tokens // 16
    for b in range(8):
        place = lax.rem(pos[2] + b, 8)
        for h in range(2):
            src = pieces[4 + h] if b == 4 else pieces[b if b < 4 else b + 1].at[h]
            row = pl.multiple_of((8 * h + place) * size, size)
            bring(src, states.at[pl.ds(row, size)])
    n_states = len(copies)
    ends = []
    for half in range(2):
        quarters, *arrived = ins[4 * half : 4 * half + 4]
        for s, src in enumerate([quarters.at[y], *arrived]):
            lanes = pl.ds(pl.multiple_of(lax.rem(y + 4 - s, 4) * width, width), width)
            bring(src, table.at[half, :, lanes])
        ends.append(len(copies))
    for copy in copies[:n_states]:
        copy.wait()

    lane = lax.broadcasted_iota(jnp.int32, (8, 128), 1)
    scale = jnp.where(lane == 0, 1.0, jnp.where(lane == 1, 256.0, jnp.where(lane == 2, 65536.0, 0.0)))
    scale = scale.astype(bf16)
    wanted = lax.dot_general(scale, states[:, full:], NT, preferred_element_type=f32)[:1].astype(jnp.int32)
    wanted_ref[...] = wanted
    total = jnp.zeros((1, tokens), f32)
    chosen = jnp.zeros((1, tokens), f32)
    tile = held.shape[1]
    outs = [pltpu.make_async_copy(states.at[:, pl.ds(pl.multiple_of(y * width, width), width)], own_ref, out_sems.at[held.shape[0]])]
    outs[0].start()
    for half in range(2):
        for copy in copies[ends[half - 1] if half else n_states : ends[half]]:
            copy.wait()
        for t in range(quarter // tile):
            rows = pl.ds(t * tile, tile)
            logits = lax.dot_general(table[half, rows], states[:, :full], NT, preferred_element_type=f32)
            capped = soft_ceiling * jnp.tanh(logits / soft_ceiling)
            k = half * (quarter // tile) + t
            held[k] = capped
            outs.append(pltpu.make_async_copy(held.at[k], capped_ref.at[pl.ds(k * tile, tile)], out_sems.at[k]))
            outs[-1].start()
            total = total + jnp.sum(jnp.exp(capped), 0, keepdims=True)
            ids = pos[4 + half] + t * tile + lax.broadcasted_iota(jnp.int32, (tile, tokens), 0)
            chosen = chosen + jnp.sum(jnp.where(ids == wanted, capped, 0.0), 0, keepdims=True)
    per = tokens // 4
    sums = [v[:, a * per : (a + 1) * per] for v in (total, chosen) for a in range(4)]
    sums_ref[...] = jnp.concatenate(sums, 0)
    for out in outs:
        out.wait()


def logits_of(pos, row_pieces, entry_pieces, width, quarter):
    tokens = 16 * row_pieces[0].shape[1]
    tile = 512
    lanes = 4 * width + 128
    return pl.pallas_call(
        logits_kernel,
        out_shape=(
            pltpu.HBM((2 * quarter, tokens), f32),
            jax.ShapeDtypeStruct((8, 128), f32),
            jax.ShapeDtypeStruct((1, tokens), jnp.int32),
            jax.ShapeDtypeStruct((tokens, width), bf16),
        ),
        in_specs=[pl.BlockSpec(memory_space=pltpu.SMEM)]
        + [pl.BlockSpec(memory_space=pltpu.HBM)] * (len(row_pieces) + len(entry_pieces)),
        out_specs=(
            pl.BlockSpec(memory_space=pltpu.HBM),
            pl.BlockSpec(memory_space=VM),
            pl.BlockSpec(memory_space=VM),
            pl.BlockSpec(memory_space=pltpu.HBM),
        ),
        scratch_shapes=[
            VM((tokens, lanes), bf16),
            VM((2, quarter, 4 * width), bf16),
            VM((2 * quarter // tile, tile, tokens), f32),
            pltpu.SemaphoreType.DMA((24,)),
            pltpu.SemaphoreType.DMA((2 * quarter // tile + 1,)),
        ],
        compiler_params=limit(26),
        cost_estimate=pl.CostEstimate(
            flops=2 * 2 * quarter * tokens * 4 * width, bytes_accessed=13 << 20, transcendentals=4 * quarter * tokens
        ),
    )(pos, *in_hbm(*row_pieces, *entry_pieces))


def logit_grad(capped, totals, ids, wanted):
    ratio = capped / soft_ceiling
    share = jnp.exp(capped) / totals - jnp.where(ids == wanted, 1.0, 0.0)
    return (share * (1.0 - ratio * ratio)).astype(bf16)


def grad_kernel(half, pos, got, capped_ref, wanted_ref, sums_ref, *outs):
    sums = got[0]
    for k in range(1, got.shape[0]):
        sums = sums + got[k]
    sums_ref[...] = sums
    tile, wide = capped_ref.shape
    start = pl.program_id(0) * tile
    first = jnp.where(start < half, pos[4], pos[5] - half) + start
    ids = first + lax.broadcasted_iota(jnp.int32, (tile, 128), 0)
    for at in range(0, wide, 128):
        row = at // 128
        wanted = wanted_ref[:, at : at + 128]
        out = outs[2 * at // wide]
        put = at % (wide // 2)
        out[:, put : put + 128] = logit_grad(capped_ref[:, at : at + 128], sums[row : row + 1], ids, wanted)


def grad_of(pos, got, capped, wanted):
    entries, wide = capped.shape
    tile = entries // 2
    return pl.pallas_call(
        functools.partial(grad_kernel, entries // 2),
        grid=(entries // tile,),
        out_shape=(jax.ShapeDtypeStruct((8, 128), f32),) + (jax.ShapeDtypeStruct((entries, wide // 2), bf16),) * 2,
        in_specs=[
            pl.BlockSpec(memory_space=pltpu.SMEM),
            pl.BlockSpec(got.shape, lambda i: (0, 0, 0)),
            pl.BlockSpec((tile, wide), lambda i: (i, 0)),
            pl.BlockSpec(wanted.shape, lambda i: (0, 0)),
        ],
        out_specs=(pl.BlockSpec((8, 128), lambda i: (0, 0)),) + (pl.BlockSpec((tile, wide // 2), lambda i: (i, 0)),) * 2,
        compiler_params=limit(16),
        cost_estimate=pl.CostEstimate(flops=8 * entries * wide, bytes_accessed=3 << 20, transcendentals=entries * wide),
    )(pos, got, *in_hbm(capped), wanted)


def pack_kernel(*refs):
    ins, out, sems = refs[:-2], refs[-2], refs[-1]
    half = ins[0].shape[0] // 2
    copies = []
    for s, ref in enumerate(ins):
        copies.append(pltpu.make_async_copy(ref.at[pl.ds(half, half)], out.at[pl.ds(s * half, half)], sems.at[s]))
        copies[-1].start()
    for copy in copies:
        copy.wait()


def lower_halves(pieces):
    rows, wide = pieces[0].shape
    return pl.pallas_call(
        pack_kernel,
        out_shape=jax.ShapeDtypeStruct((len(pieces) * rows // 2, wide), bf16),
        in_specs=[pl.BlockSpec(memory_space=pltpu.HBM)] * len(pieces),
        out_specs=pl.BlockSpec(memory_space=pltpu.HBM),
        scratch_shapes=[pltpu.SemaphoreType.DMA((len(pieces),))],
        compiler_params=limit(1),
        cost_estimate=pl.CostEstimate(flops=0, bytes_accessed=1 << 16, transcendentals=0),
    )(*in_hbm(*pieces))


def table_kernel(pos, own_states, beside_states, *refs):
    moved, lower, (out, grads, states, result, sems, out_sems) = refs[:8], refs[8:10], refs[10:]
    tokens, width = own_states.shape
    quarter = grads.shape[1]
    copies = []

    def bring(src, dst):
        copy = pltpu.make_async_copy(src, dst, sems.at[len(copies)])
        copies.append(copy)
        copy.start()

    bring(own_states, states.at[pl.ds(0, tokens)])
    bring(beside_states, states.at[pl.ds(tokens, tokens)])
    for s in range(4):
        for h in range(2):
            wide = tokens // 2
            bring(moved[4 * h + s].at[pl.ds(0, quarter)], grads.at[s, :, pl.ds(h * wide, wide)])
            bring(lower[h].at[pl.ds(s * quarter, quarter)], grads.at[s, :, pl.ds(tokens + h * wide, wide)])
    for copy in copies[:2]:
        copy.wait()
    outs = [None, None]
    tile = 256
    for s in range(4):
        for copy in copies[2 + 4 * s : 6 + 4 * s]:
            copy.wait()
        slot = s % 2
        if outs[slot] is not None:
            outs[slot].wait()

        @pl.loop(0, quarter // tile)
        def _(i):
            rows = pl.ds(pl.multiple_of(i * tile, tile), tile)
            result[slot, rows, :] = jnp.dot(grads[s, rows, :], states[...], preferred_element_type=f32)

        at = pl.multiple_of(lax.rem(pos[1] + 4 - s, 4) * quarter, quarter)
        outs[slot] = pltpu.make_async_copy(result.at[slot], out.at[pl.ds(at, quarter)], out_sems.at[slot])
        outs[slot].start()
    for copy in outs:
        copy.wait()


def table_grad_of(pos, own_states, beside_states, pieces, entries):
    tokens, width = own_states.shape
    quarter = entries // 4
    return pl.pallas_call(
        table_kernel,
        out_shape=jax.ShapeDtypeStruct((entries, width), f32),
        in_specs=[pl.BlockSpec(memory_space=pltpu.SMEM)] + [pl.BlockSpec(memory_space=pltpu.HBM)] * (2 + len(pieces)),
        out_specs=pl.BlockSpec(memory_space=pltpu.HBM),
        scratch_shapes=[
            VM((4, quarter, 2 * tokens), bf16),
            VM((2 * tokens, width), bf16),
            VM((2, quarter, width), f32),
            pltpu.SemaphoreType.DMA((18,)),
            pltpu.SemaphoreType.DMA((2,)),
        ],
        compiler_params=limit(20),
        cost_estimate=pl.CostEstimate(flops=1 << 20, bytes_accessed=1 << 18, transcendentals=0),
    )(pos, *in_hbm(own_states, beside_states, *pieces))


def local(hidden_states, embedding, targets):
    z, x, c, y = (lax.axis_index(a) for a in ("z", "x", "c", "y"))
    rows, width = hidden_states.shape
    entries = embedding.shape[0]
    quarter = entries // 4
    tokens = 32 * rows
    chip = (z * 4 + x) * 2
    first = [(chip + c) * entries + y * quarter, (chip + 1 - c) * entries + y * quarter]
    pos = jnp.stack([x, y, z, c, *first]).astype(jnp.int32)

    digits = jnp.stack([targets & 255, (targets >> 8) & 255, targets >> 16], 1).astype(bf16)
    block = jnp.concatenate([hidden_states, jnp.pad(digits, ((0, 0), (0, 125)))], 1)
    got = lax.all_to_all(jnp.broadcast_to(block, (16, *block.shape)), ("x", "y"), 0, 0, tiled=True)

    quarters = embedding.reshape(4, quarter, width)
    beside = beside_of(embedding).reshape(4, quarter, width)

    def quarter_at(q, k):
        return lax.dynamic_index_in_dim(q, (y + k) % 4, 0, False)

    own = {s: over(quarter_at(quarters, s), "y", 4, s) for s in (1, 3)}

    got = got.reshape(4, 4, 2, rows // 2, width + 128).transpose(2, 0, 1, 3, 4)
    at_x = jnp.concatenate([got[:, :, k, :, :width] for k in range(4)] + [got[:, :, 0, :, width:]], 3)
    at_x = at_x.reshape(2, 2 * rows, -1)
    up, down = [at_x], [at_x]
    for k in range(3):
        up.append(over(up[-1], "z", 8, -1))
        down.append(over(down[-1], "z", 8, 1))
        if k == 1:
            up[-1], down[-1], own[1], own[3] = tie(up[-1], down[-1], own[1], own[3])
            send, own[1], own[3] = tie(quarter_at(quarters, 2), own[1], own[3])
            own[2] = over(send, "y", 4, 2)
    far = [over(up[3][0], "z", 8, -1), over(down[3][1], "z", 8, 1)]
    own[2], *far = tie(own[2], *far)
    other = {s: beside_of(own[s]) for s in (1, 3, 2)}
    row_pieces = [*up, *far, down[3], down[2], down[1]]

    entry_pieces = (quarters, own[1], own[2], own[3], beside, other[1], other[2], other[3])
    capped, sums, wanted, own_states = logits_of(pos, row_pieces, entry_pieces, width, quarter)

    got = lax.all_to_all(jnp.broadcast_to(sums, (16, *sums.shape)), ("x", "y"), 0, 0, tiled=True)
    sums = jnp.sum(got, 0)
    got = lax.all_to_all(jnp.broadcast_to(sums, (8, *sums.shape)), "z", 0, 0, tiled=True)
    sums, *grad = grad_of(pos, got, capped, wanted)
    beside_states = beside_of(own_states)
    moved = [[grad[0]] + [over(grad[0], "y", 4, s) for s in (1, 2, 3)]]
    grad[1], *moved[0][1:] = tie(grad[1], *moved[0][1:])
    moved.append([grad[1]] + [over(grad[1], "y", 4, s) for s in (1, 2, 3)])

    def back(pieces):
        part = None
        for s in (0, 1, 3, 2):
            term = lax.dot_general(pieces[s], both[s], (((0,), (0,)), ((), ())), preferred_element_type=f32)
            part = term if part is None else part + term
        return part.astype(bf16).reshape(32, rows // 2, width)

    late, beside_late, moved[0][0] = tie(quarters, beside, moved[0][0])
    both = [jnp.concatenate([quarter_at(late, -s), quarter_at(beside_late, -s)]) for s in range(4)]
    home = [back(moved[0])]
    got = [lax.all_to_all(home[0], ("z", "x"), 0, 0, tiled=True)]
    moved[1][2], home[0] = tie(moved[1][2], home[0])
    home.append(back(moved[1]))
    home[1], got[0] = tie(home[1], got[0])
    got.append(lax.all_to_all(home[1], ("z", "x"), 0, 0, tiled=True))
    for k in range(2):
        *moved[k], home[k] = tie(*moved[k], home[k])
    lower = [beside_of(lower_halves(pieces)) for pieces in moved]
    table_grad = table_grad_of(pos, own_states, beside_states, [*moved[0], *moved[1], *lower], entries)
    got[1], table_grad = tie(got[1], table_grad)
    hidden_grad = jnp.concatenate([jnp.sum(v.astype(f32), 0) for v in got], 0)

    terms = jnp.sum(jnp.log(sums[:4]) - sums[4:])
    loss = (terms + beside_of(terms)) / (2 * tokens)

    return (loss, hidden_grad, table_grad)


def solution(mesh):
    cut = Mesh(mesh.devices.reshape(8, 4, 2, 4), ("z", "x", "c", "y"))
    vocab = ("z", "x", "c")
    placed = (P(vocab, "y"), P(vocab, "y"), P(vocab))
    return jax.shard_map(
        local,
        mesh=cut,
        in_specs=placed,
        out_specs=(P(), P(vocab, "y"), P(vocab, "y")),
        check_vma=False,
    )
```

```python
import functools

import jax
import jax.numpy as jnp
from jax import lax
from jax.experimental import pallas as pl
from jax.experimental.pallas import tpu as pltpu
from jax.sharding import Mesh, PartitionSpec as P

soft_ceiling = 30.0
swap = [(0, 1), (1, 0)]
f32, bf16 = jnp.float32, jnp.bfloat16
VM = pltpu.VMEM
NT = (((1,), (1,)), ((), ()))

def over(value, axis, n, s):
    return lax.ppermute(value, axis, [(i, (i + s) % n) for i in range(n)])


def beside_of(value):
    return lax.ppermute(value, "c", swap)


def tie(*values):
    return lax.optimization_barrier(values)


def in_hbm(*values):
    return [pltpu.with_memory_space_constraint(v, pltpu.HBM) for v in values]


def limit(mib):
    return pltpu.CompilerParams(vmem_limit_bytes=mib << 20)


def logits_kernel(pos, *refs):
    pieces, ins = refs[:9], refs[9:17]
    capped_ref, sums_ref, wanted_ref, own_ref, states, table, held, sems, out_sems = refs[17:]
    quarter, full = table.shape[1:]
    width = full // 4
    tokens = states.shape[0]
    copies = []

    def bring(src, dst):
        copy = pltpu.make_async_copy(src, dst, sems.at[len(copies)])
        copies.append(copy)
        copy.start()

    y = pos[1]
    size = tokens // 16
    for b in range(8):
        place = lax.rem(pos[2] + b, 8)
        for h in range(2):
            src = pieces[4 + h] if b == 4 else pieces[b if b < 4 else b + 1].at[h]
            row = pl.multiple_of((8 * h + place) * size, size)
            bring(src, states.at[pl.ds(row, size)])
    n_states = len(copies)
    ends = []
    for half in range(2):
        quarters, *arrived = ins[4 * half : 4 * half + 4]
        for s, src in enumerate([quarters.at[y], *arrived]):
            lanes = pl.ds(pl.multiple_of(lax.rem(y + 4 - s, 4) * width, width), width)
            bring(src, table.at[half, :, lanes])
        ends.append(len(copies))
    for copy in copies[:n_states]:
        copy.wait()

    lane = lax.broadcasted_iota(jnp.int32, (8, 128), 1)
    scale = jnp.where(lane == 0, 1.0, jnp.where(lane == 1, 256.0, jnp.where(lane == 2, 65536.0, 0.0)))
    scale = scale.astype(bf16)
    wanted = lax.dot_general(scale, states[:, full:], NT, preferred_element_type=f32)[:1].astype(jnp.int32)
    wanted_ref[...] = wanted
    total = jnp.zeros((1, tokens), f32)
    chosen = jnp.zeros((1, tokens), f32)
    tile = held.shape[1]
    outs = [pltpu.make_async_copy(states.at[:, pl.ds(pl.multiple_of(y * width, width), width)], own_ref, out_sems.at[held.shape[0]])]
    outs[0].start()
    for half in range(2):
        for copy in copies[ends[half - 1] if half else n_states : ends[half]]:
            copy.wait()
        for t in range(quarter // tile):
            rows = pl.ds(t * tile, tile)
            logits = lax.dot_general(table[half, rows], states[:, :full], NT, preferred_element_type=f32)
            capped = soft_ceiling * jnp.tanh(logits / soft_ceiling)
            k = half * (quarter // tile) + t
            held[k] = capped
            outs.append(pltpu.make_async_copy(held.at[k], capped_ref.at[pl.ds(k * tile, tile)], out_sems.at[k]))
            outs[-1].start()
            total = total + jnp.sum(jnp.exp(capped), 0, keepdims=True)
            ids = pos[4 + half] + t * tile + lax.broadcasted_iota(jnp.int32, (tile, tokens), 0)
            chosen = chosen + jnp.sum(jnp.where(ids == wanted, capped, 0.0), 0, keepdims=True)
    per = tokens // 4
    sums = [v[:, a * per : (a + 1) * per] for v in (total, chosen) for a in range(4)]
    sums_ref[...] = jnp.concatenate(sums, 0)
    for out in outs:
        out.wait()


def logits_of(pos, row_pieces, entry_pieces, width, quarter):
    tokens = 16 * row_pieces[0].shape[1]
    tile = 512
    lanes = 4 * width + 128
    return pl.pallas_call(
        logits_kernel,
        out_shape=(
            pltpu.HBM((2 * quarter, tokens), f32),
            jax.ShapeDtypeStruct((8, 128), f32),
            jax.ShapeDtypeStruct((1, tokens), jnp.int32),
            jax.ShapeDtypeStruct((tokens, width), bf16),
        ),
        in_specs=[pl.BlockSpec(memory_space=pltpu.SMEM)]
        + [pl.BlockSpec(memory_space=pltpu.HBM)] * (len(row_pieces) + len(entry_pieces)),
        out_specs=(
            pl.BlockSpec(memory_space=pltpu.HBM),
            pl.BlockSpec(memory_space=VM),
            pl.BlockSpec(memory_space=VM),
            pl.BlockSpec(memory_space=pltpu.HBM),
        ),
        scratch_shapes=[
            VM((tokens, lanes), bf16),
            VM((2, quarter, 4 * width), bf16),
            VM((2 * quarter // tile, tile, tokens), f32),
            pltpu.SemaphoreType.DMA((24,)),
            pltpu.SemaphoreType.DMA((2 * quarter // tile + 1,)),
        ],
        compiler_params=limit(26),
        cost_estimate=pl.CostEstimate(
            flops=2 * 2 * quarter * tokens * 4 * width, bytes_accessed=13 << 20, transcendentals=4 * quarter * tokens
        ),
    )(pos, *in_hbm(*row_pieces, *entry_pieces))


def logit_grad(capped, totals, ids, wanted):
    ratio = capped / soft_ceiling
    share = jnp.exp(capped) / totals - jnp.where(ids == wanted, 1.0, 0.0)
    return (share * (1.0 - ratio * ratio)).astype(bf16)


def grad_kernel(half, pos, got, capped_ref, wanted_ref, sums_ref, *outs):
    sums = got[0]
    for k in range(1, got.shape[0]):
        sums = sums + got[k]
    sums_ref[...] = sums
    tile, wide = capped_ref.shape
    start = pl.program_id(0) * tile
    first = jnp.where(start < half, pos[4], pos[5] - half) + start
    ids = first + lax.broadcasted_iota(jnp.int32, (tile, 128), 0)
    for at in range(0, wide, 128):
        row = at // 128
        wanted = wanted_ref[:, at : at + 128]
        out = outs[2 * at // wide]
        put = at % (wide // 2)
        out[:, put : put + 128] = logit_grad(capped_ref[:, at : at + 128], sums[row : row + 1], ids, wanted)


def grad_of(pos, got, capped, wanted):
    entries, wide = capped.shape
    tile = entries // 2
    return pl.pallas_call(
        functools.partial(grad_kernel, entries // 2),
        grid=(entries // tile,),
        out_shape=(jax.ShapeDtypeStruct((8, 128), f32),) + (jax.ShapeDtypeStruct((entries, wide // 2), bf16),) * 2,
        in_specs=[
            pl.BlockSpec(memory_space=pltpu.SMEM),
            pl.BlockSpec(got.shape, lambda i: (0, 0, 0)),
            pl.BlockSpec((tile, wide), lambda i: (i, 0)),
            pl.BlockSpec(wanted.shape, lambda i: (0, 0)),
        ],
        out_specs=(pl.BlockSpec((8, 128), lambda i: (0, 0)),) + (pl.BlockSpec((tile, wide // 2), lambda i: (i, 0)),) * 2,
        compiler_params=limit(16),
        cost_estimate=pl.CostEstimate(flops=8 * entries * wide, bytes_accessed=3 << 20, transcendentals=entries * wide),
    )(pos, got, *in_hbm(capped), wanted)


def pack_kernel(*refs):
    ins, out, sems = refs[:-2], refs[-2], refs[-1]
    half = ins[0].shape[0] // 2
    copies = []
    for s, ref in enumerate(ins):
        copies.append(pltpu.make_async_copy(ref.at[pl.ds(half, half)], out.at[pl.ds(s * half, half)], sems.at[s]))
        copies[-1].start()
    for copy in copies:
        copy.wait()


def lower_halves(pieces):
    rows, wide = pieces[0].shape
    return pl.pallas_call(
        pack_kernel,
        out_shape=jax.ShapeDtypeStruct((len(pieces) * rows // 2, wide), bf16),
        in_specs=[pl.BlockSpec(memory_space=pltpu.HBM)] * len(pieces),
        out_specs=pl.BlockSpec(memory_space=pltpu.HBM),
        scratch_shapes=[pltpu.SemaphoreType.DMA((len(pieces),))],
        compiler_params=limit(1),
        cost_estimate=pl.CostEstimate(flops=0, bytes_accessed=1 << 16, transcendentals=0),
    )(*in_hbm(*pieces))


def table_kernel(pos, own_states, beside_states, *refs):
    moved, lower, (out, grads, states, result, sems, out_sems) = refs[:8], refs[8:10], refs[10:]
    tokens, width = own_states.shape
    quarter = grads.shape[1]
    copies = []

    def bring(src, dst):
        copy = pltpu.make_async_copy(src, dst, sems.at[len(copies)])
        copies.append(copy)
        copy.start()

    bring(own_states, states.at[pl.ds(0, tokens)])
    bring(beside_states, states.at[pl.ds(tokens, tokens)])
    for s in range(4):
        for h in range(2):
            wide = tokens // 2
            bring(moved[4 * h + s].at[pl.ds(0, quarter)], grads.at[s, :, pl.ds(h * wide, wide)])
            bring(lower[h].at[pl.ds(s * quarter, quarter)], grads.at[s, :, pl.ds(tokens + h * wide, wide)])
    for copy in copies[:2]:
        copy.wait()
    outs = [None, None]
    tile = 256
    for s in range(4):
        for copy in copies[2 + 4 * s : 6 + 4 * s]:
            copy.wait()
        slot = s % 2
        if outs[slot] is not None:
            outs[slot].wait()

        @pl.loop(0, quarter // tile)
        def _(i):
            rows = pl.ds(pl.multiple_of(i * tile, tile), tile)
            result[slot, rows, :] = jnp.dot(grads[s, rows, :], states[...], preferred_element_type=f32)

        at = pl.multiple_of(lax.rem(pos[1] + 4 - s, 4) * quarter, quarter)
        outs[slot] = pltpu.make_async_copy(result.at[slot], out.at[pl.ds(at, quarter)], out_sems.at[slot])
        outs[slot].start()
    for copy in outs:
        copy.wait()


def table_grad_of(pos, own_states, beside_states, pieces, entries):
    tokens, width = own_states.shape
    quarter = entries // 4
    return pl.pallas_call(
        table_kernel,
        out_shape=jax.ShapeDtypeStruct((entries, width), f32),
        in_specs=[pl.BlockSpec(memory_space=pltpu.SMEM)] + [pl.BlockSpec(memory_space=pltpu.HBM)] * (2 + len(pieces)),
        out_specs=pl.BlockSpec(memory_space=pltpu.HBM),
        scratch_shapes=[
            VM((4, quarter, 2 * tokens), bf16),
            VM((2 * tokens, width), bf16),
            VM((2, quarter, width), f32),
            pltpu.SemaphoreType.DMA((18,)),
            pltpu.SemaphoreType.DMA((2,)),
        ],
        compiler_params=limit(20),
        cost_estimate=pl.CostEstimate(flops=1 << 20, bytes_accessed=1 << 18, transcendentals=0),
    )(pos, *in_hbm(own_states, beside_states, *pieces))


def local(hidden_states, embedding, targets):
    z, x, c, y = (lax.axis_index(a) for a in ("z", "x", "c", "y"))
    rows, width = hidden_states.shape
    entries = embedding.shape[0]
    quarter = entries // 4
    tokens = 32 * rows
    chip = (z * 4 + x) * 2
    first = [(chip + c) * entries + y * quarter, (chip + 1 - c) * entries + y * quarter]
    pos = jnp.stack([x, y, z, c, *first]).astype(jnp.int32)

    digits = jnp.stack([targets & 255, (targets >> 8) & 255, targets >> 16], 1).astype(bf16)
    block = jnp.concatenate([hidden_states, jnp.pad(digits, ((0, 0), (0, 125)))], 1)
    got = lax.all_to_all(jnp.broadcast_to(block, (16, *block.shape)), ("x", "y"), 0, 0, tiled=True)

    quarters = embedding.reshape(4, quarter, width)
    beside = beside_of(embedding).reshape(4, quarter, width)

    def quarter_at(q, k):
        return lax.dynamic_index_in_dim(q, (y + k) % 4, 0, False)

    own = {s: over(quarter_at(quarters, s), "y", 4, s) for s in (1, 3)}

    got = got.reshape(4, 4, 2, rows // 2, width + 128).transpose(2, 0, 1, 3, 4)
    at_x = jnp.concatenate([got[:, :, k, :, :width] for k in range(4)] + [got[:, :, 0, :, width:]], 3)
    at_x = at_x.reshape(2, 2 * rows, -1)
    up, down = [at_x], [at_x]
    for k in range(3):
        up.append(over(up[-1], "z", 8, -1))
        down.append(over(down[-1], "z", 8, 1))
        if k == 1:
            up[-1], down[-1], own[1], own[3] = tie(up[-1], down[-1], own[1], own[3])
            send, own[1], own[3] = tie(quarter_at(quarters, 2), own[1], own[3])
            own[2] = over(send, "y", 4, 2)
    far = [over(up[3][0], "z", 8, -1), over(down[3][1], "z", 8, 1)]
    own[2], *far = tie(own[2], *far)
    other = {s: beside_of(own[s]) for s in (1, 3, 2)}
    row_pieces = [*up, *far, down[3], down[2], down[1]]

    entry_pieces = (quarters, own[1], own[2], own[3], beside, other[1], other[2], other[3])
    capped, sums, wanted, own_states = logits_of(pos, row_pieces, entry_pieces, width, quarter)

    got = lax.all_to_all(jnp.broadcast_to(sums, (16, *sums.shape)), ("x", "y"), 0, 0, tiled=True)
    sums = jnp.sum(got, 0)
    got = lax.all_to_all(jnp.broadcast_to(sums, (8, *sums.shape)), "z", 0, 0, tiled=True)
    sums, *grad = grad_of(pos, got, capped, wanted)
    beside_states = beside_of(own_states)
    moved = [[grad[0]] + [over(grad[0], "y", 4, s) for s in (1, 2, 3)]]
    grad[1], *moved[0][1:] = tie(grad[1], *moved[0][1:])
    moved.append([grad[1]] + [over(grad[1], "y", 4, s) for s in (1, 2, 3)])

    def back(pieces):
        part = None
        for s in (0, 1, 3, 2):
            term = lax.dot_general(pieces[s], both[s], (((0,), (0,)), ((), ())), preferred_element_type=f32)
            part = term if part is None else part + term
        return part.astype(bf16).reshape(32, rows // 2, width)

    late, beside_late, moved[0][0] = tie(quarters, beside, moved[0][0])
    both = [jnp.concatenate([quarter_at(late, -s), quarter_at(beside_late, -s)]) for s in range(4)]
    terms = jnp.sum(jnp.log(sums[:4]) - sums[4:])
    loss = (terms + beside_of(terms)) / (2 * tokens)
    home = [back(moved[0])]
    got = [lax.all_to_all(home[0], ("z", "x"), 0, 0, tiled=True)]
    moved[1][2], home[0], loss = tie(moved[1][2], home[0], loss)
    home.append(back(moved[1]))
    home[1], got[0] = tie(home[1], got[0])
    got.append(lax.all_to_all(home[1], ("z", "x"), 0, 0, tiled=True))
    for k in range(2):
        *moved[k], home[k] = tie(*moved[k], home[k])
    lower = [beside_of(lower_halves(pieces)) for pieces in moved]
    table_grad = table_grad_of(pos, own_states, beside_states, [*moved[0], *moved[1], *lower], entries)
    got[1], table_grad = tie(got[1], table_grad)
    hidden_grad = jnp.concatenate([jnp.sum(v.astype(f32), 0) for v in got], 0)

    return (loss, hidden_grad, table_grad)


def solution(mesh):
    cut = Mesh(mesh.devices.reshape(8, 4, 2, 4), ("z", "x", "c", "y"))
    vocab = ("z", "x", "c")
    placed = (P(vocab, "y"), P(vocab, "y"), P(vocab))
    return jax.shard_map(
        local,
        mesh=cut,
        in_specs=placed,
        out_specs=(P(), P(vocab, "y"), P(vocab, "y")),
        check_vma=False,
    )
```
